32 devices in a mesh: dp: 2 (over x), row: 4 (over y, core), col: 4 (over z).
Axes of the slice: x: 2, y: 2, z: 4, core: 2. Of those that a mesh axis runs over, the one named last changes fastest.
Arguments:
- inputs: bfloat16 [8192, 1024], P(('dp', 'row'), 'col'), may hold values from -29 to 29
- query_weight: bfloat16 [1024, 1024], P('col', 'row'), may hold values from -0.1875 to 0.1875
- query_bias: float32 [1024], P('row'), may hold values from -3 to 3
- key_weight: bfloat16 [1024, 1024], P('col', 'row'), may hold values from -0.1875 to 0.1875
- value_weight: bfloat16 [1024, 1024], P('col', 'row'), may hold values from -0.1875 to 0.1875
- value_bias: float32 [1024], P('row'), may hold values from -0.3 to 0.3
- mixer_weight: bfloat16 [1024, 1024], P('row', 'col'), may hold values from -2 to 2
- mixer_bias: float32 [1024], P('col'), may hold values from -2 to 2
- norm_gain: float32 [1024], P('col'), may hold values from 0.4 to 2.3
- norm_bias: float32 [1024], P('col'), may hold values from -2 to 2
- inner_weight: bfloat16 [1024, 4096], P('col', 'row'), may hold values from -0.1875 to 0.1875
- inner_bias: float32 [4096], P('row'), may hold values from -2 to 2
- outer_weight: bfloat16 [4096, 1024], P('row', 'col'), may hold values from -0.09375 to 0.09375
- outer_bias: float32 [1024], P('col'), may hold values from -2 to 2
- final_gain: float32 [1024], P('col'), may hold values from 0.25 to 1.75
- final_bias: float32 [1024], P('col'), may hold values from -2 to 2
- cotangent: bfloat16 [8192, 1024], P(('dp', 'row'), 'col'), may hold values from -6 to 6
Outputs:
- layer_out: bfloat16 [8192, 1024], P(('dp', 'row'), 'col')
- grad_inputs: float32 [8192, 1024], P(('dp', 'row'), 'col')
- grad_queryweight: float32 [1024, 1024], P('col', 'row')
- grad_querybias: float32 [1024], P('row')
- grad_keyweight: float32 [1024, 1024], P('col', 'row')
- grad_valueweight: float32 [1024, 1024], P('col', 'row')
- grad_valuebias: float32 [1024], P('row')
- grad_mixerweight: float32 [1024, 1024], P('row', 'col')
- grad_mixerbias: float32 [1024], P('col')
- grad_normgain: float32 [1024], P('col')
- grad_normbias: float32 [1024], P('col')
- grad_innerweight: float32 [1024, 4096], P('col', 'row')
- grad_innerbias: float32 [4096], P('row')
- grad_outerweight: float32 [4096, 1024], P('row', 'col')
- grad_outerbias: float32 [1024], P('col')
- grad_finalgain: float32 [1024], P('col')
- grad_finalbias: float32 [1024], P('col')
The draws below stay inside these ranges and needn't reach their ends.
All inputs are finite; a program needn't handle non-finite values.
Results may differ from the reference program's by a relative error of at most 0.01065.
The reference program's roundings to bfloat16 on the way count: a program that leaves them out, or rounds other values in their place, can miss the bound.
Values may be sent and summed in bfloat16 or wider, within the bound.
A program may use at most 128 MiB of HBM per device.

```python
import math
import jax
import jax.numpy as jnp
from jax import lax

D = 1024
H = 16
DH = 64
FF = 4096
L = 512
TOKENS = 8192


def draw_inputs(key, part):
    key = jax.random.fold_in(key, 11)
    base_key, rough_key = jax.random.split(key, 2)
    ramp = jnp.exp(jnp.arange(D, dtype=jnp.float32) * (math.log(3.0) / D))
    rough = jax.random.uniform(rough_key, (D,), jnp.float32, 0.7, 1.4)
    base = jnp.clip(jax.random.normal(base_key, (TOKENS, D), jnp.float32), -6.0, 6.0)
    return (base * ramp * rough).astype(jnp.bfloat16)


def draw_norm_gain(key, part):
    key = jax.random.fold_in(key, 23)
    ramp = 0.6 * jnp.exp(jnp.arange(D, dtype=jnp.float32) * (math.log(3.0) / D))
    rough = jax.random.uniform(key, (D,), jnp.float32, 0.85, 1.15)
    return (ramp * rough).astype(jnp.float32)


def steps_of(key, extent, cuts, least, largest):
    level = 1.0
    for axis_at, shards_of in cuts:
        heights = jax.random.uniform(jax.random.fold_in(jax.random.fold_in(key, 6), axis_at), (shards_of,), jnp.float32, least / len(cuts), largest / len(cuts))
        level = level * jnp.repeat(jnp.exp(heights), extent[axis_at] // shards_of).reshape((-1,) + (1,) * (len(extent) - 1 - axis_at))
    return level


def scatter_about(stream_key, extent, width, bound, cuts=(), kind=jnp.bfloat16):
    values = jax.random.normal(stream_key, extent, jnp.float32) * width
    if len(cuts) > 0:
        values = steps_of(stream_key, extent, cuts, -0.22, 0.18) * values
    return jnp.clip(values, min=-bound, max=bound).astype(kind)


def setup_inputs(seed: int = 0) -> dict:
    streams_of = jax.random.split(jax.random.key(seed), 18)
    inputs = draw_inputs(jax.random.fold_in(streams_of[17], 71), 0)
    query_weight = scatter_about(streams_of[1], (D, D), D ** -0.5, 0.1875, ((0, 4), (1, 4)))
    query_bias = scatter_about(streams_of[2], (D,), 0.5, 3.0, ((0, 4),), jnp.float32)
    key_weight = scatter_about(streams_of[3], (D, D), D ** -0.5, 0.1875, ((0, 4), (1, 4)))
    value_weight = scatter_about(streams_of[4], (D, D), D ** -0.5, 0.1875, ((0, 4), (1, 4)))
    value_bias = scatter_about(streams_of[5], (D,), 0.05, 0.3, ((0, 4),), jnp.float32)
    mixer_weight = scatter_about(streams_of[6], (D, D), (4 * D // L) ** -0.5, 2.0, ((0, 4), (1, 4)))
    mixer_bias = scatter_about(streams_of[7], (D,), 0.3, 2.0, ((0, 4),), jnp.float32)
    norm_gain = draw_norm_gain(jax.random.fold_in(streams_of[17], 71), 0)
    norm_bias = scatter_about(streams_of[9], (D,), 0.3, 2.0, ((0, 4),), jnp.float32)
    inner_weight = scatter_about(streams_of[10], (D, FF), D ** -0.5, 0.1875, ((0, 4), (1, 4)))
    inner_bias = scatter_about(streams_of[11], (FF,), 0.3, 2.0, ((0, 4),), jnp.float32)
    outer_weight = scatter_about(streams_of[12], (FF, D), FF ** -0.5, 0.09375, ((0, 4), (1, 4)))
    outer_bias = scatter_about(streams_of[13], (D,), 0.3, 2.0, ((0, 4),), jnp.float32)
    final_gain = jnp.clip(1.0 + 0.15 * jax.random.normal(streams_of[14], (D,), jnp.float32), 0.25, 1.75)
    final_bias = scatter_about(streams_of[15], (D,), 0.3, 2.0, ((0, 4),), jnp.float32)
    cotangent = scatter_about(streams_of[16], (TOKENS, D), 1.0, 6.0, ((0, 8), (1, 4)))
    return dict(inputs=inputs, query_weight=query_weight, query_bias=query_bias, key_weight=key_weight, value_weight=value_weight, value_bias=value_bias, mixer_weight=mixer_weight, mixer_bias=mixer_bias, norm_gain=norm_gain, norm_bias=norm_bias, inner_weight=inner_weight, inner_bias=inner_bias, outer_weight=outer_weight, outer_bias=outer_bias, final_gain=final_gain, final_bias=final_bias, cotangent=cotangent)


@jax.custom_vjp
def low(v):
    return lax.optimization_barrier(v.astype(jnp.bfloat16)).astype(jnp.float32)

@jax.custom_vjp
def low_back(v):
    return v

def low_keep(v):
    return (low(v), None)

def low_pass(kept, grad):
    return (grad,)

def back_keep(v):
    return (v, None)

def back_low(kept, grad):
    return (low(grad),)
low.defvjp(low_keep, low_pass)
low_back.defvjp(back_keep, back_low)
norm_eps = 1e-12

def product(left, right):
    return jnp.dot(left, right, precision=lax.Precision.HIGHEST)

def layer_norm(total, gain, shift):
    center = total - lax.optimization_barrier(jnp.mean(total, axis=-1, keepdims=True))
    spread = lax.optimization_barrier(jnp.mean(center * center, axis=-1, keepdims=True))
    return center * lax.rsqrt(spread + norm_eps) * gain + shift

def split_heads(array):
    return array.reshape(-1, L, H, DH)

def attend_one(pieces):
    query_part, key_part, value_part = pieces
    scores = jnp.einsum('qhd,khd->hqk', query_part, key_part, precision=lax.Precision.HIGHEST) * DH ** (-0.5)
    scores = low_back(scores)
    probs = jax.nn.softmax(scores, axis=-1)
    return jnp.einsum('hqk,khd->qhd', low(probs), value_part, precision=lax.Precision.HIGHEST)

def forward(inputs, query_weight, query_bias, key_weight, value_weight, value_bias, mixer_weight, mixer_bias, norm_gain, norm_bias, inner_weight, inner_bias, outer_weight, outer_bias, final_gain, final_bias):
    queries = low(low_back(product(inputs, query_weight) + query_bias))
    keys_proj = low(low_back(product(inputs, key_weight)))
    values_proj = low(low_back(product(inputs, value_weight) + value_bias))
    context = lax.map(jax.checkpoint(attend_one), (split_heads(queries), split_heads(keys_proj), split_heads(values_proj)))
    context = low(low_back(context.reshape(-1, D)))
    first_sum = inputs + low_back(product(context, mixer_weight) + mixer_bias)
    first_out = layer_norm(first_sum, norm_gain, norm_bias)
    inner_pre = low_back(product(low(first_out), inner_weight) + inner_bias)
    activated = low(jax.nn.gelu(inner_pre, approximate=False))
    second_sum = first_out + low_back(product(activated, outer_weight) + outer_bias)
    return layer_norm(second_sum, final_gain, final_bias)

def reference(inputs, query_weight, query_bias, key_weight, value_weight, value_bias, mixer_weight, mixer_bias, norm_gain, norm_bias, inner_weight, inner_bias, outer_weight, outer_bias, final_gain, final_bias, cotangent):
    floats = tuple((array.astype(jnp.float32) for array in (inputs, query_weight, query_bias, key_weight, value_weight, value_bias, mixer_weight, mixer_bias, norm_gain, norm_bias, inner_weight, inner_bias, outer_weight, outer_bias, final_gain, final_bias)))
    layer_value, pullback = jax.vjp(forward, *floats)
    grads = pullback(cotangent.astype(jnp.float32))
    return (layer_value.astype(jnp.bfloat16), grads[0], grads[1], grads[2], grads[3], grads[4], grads[5], grads[6], grads[7], grads[8], grads[9], grads[10], grads[11], grads[12], grads[13], grads[14], grads[15])
```

```python
import math

import jax
import jax.numpy as jnp
from jax import lax
from jax.sharding import PartitionSpec as P

D = 1024
DH = 64
L = 512


norm_eps = 1e-12


def multiply(left, right, flipped):
    if flipped:
        return lax.dot_general(
            left, right, (((1,), (1,)), ((), ())), preferred_element_type=jnp.float32
        )
    return jnp.dot(left, right, preferred_element_type=jnp.float32)


def outer_product(left, right):
    return lax.dot_general(
        left, right, (((0,), (0,)), ((), ())), preferred_element_type=jnp.float32
    )


def column_sums(block):
    return jnp.dot(
        jnp.ones((1, block.shape[0]), block.dtype), block, preferred_element_type=jnp.float32
    )[0]


def rows_gather(block):
    return lax.all_gather(block, "row", axis=0, tiled=True)


def cols_gather(block):
    return lax.all_gather(block, "col", axis=0, tiled=True)


def transposed(block):
    row_count, col_count = lax.axis_size("row"), lax.axis_size("col")
    pairs = [
        (r * col_count + c, c * col_count + r) for r in range(row_count) for c in range(col_count)
    ]
    return lax.ppermute(block, ("row", "col"), pairs)


def row_reduce(partial, dimension=0):
    return lax.psum_scatter(
        partial.astype(jnp.bfloat16), "row", scatter_dimension=dimension, tiled=True
    )


def grad_reduce(partial):
    scattered = lax.psum_scatter(
        partial.astype(jnp.bfloat16), "col", scatter_dimension=0, tiled=True
    )
    return lax.psum(scattered, "dp").astype(jnp.float32)


def normalize(total):
    center = jnp.mean(total, axis=-1, keepdims=True)
    moved = total - center
    scale = lax.rsqrt(jnp.mean(moved * moved, axis=-1, keepdims=True) + norm_eps)
    return moved * scale, scale


def norm_back(scaled_grad, normed, scale):
    first = jnp.mean(scaled_grad, axis=-1, keepdims=True)
    second = jnp.mean(scaled_grad * normed, axis=-1, keepdims=True)
    return scale * (scaled_grad - first - normed * second)


def gelu_slope(values):
    normal_cdf = 0.5 * (1.0 + jax.scipy.special.erf(values * (1.0 / math.sqrt(2.0))))
    density = jnp.exp(-0.5 * values * values) * (1.0 / math.sqrt(2.0 * math.pi))
    return normal_cdf + values * density


def split_heads(block, heads):
    return block.reshape(-1, L, heads, DH)


def attend(query_rows, key_rows, value_rows, heads):
    factor = DH ** (-0.5)
    scores = (
        jnp.einsum(
            "bqhd,bkhd->bhqk",
            split_heads(query_rows, heads),
            split_heads(key_rows, heads),
            preferred_element_type=jnp.float32,
        )
        * factor
    )
    top = jnp.max(scores, axis=-1, keepdims=True)
    weights = jnp.exp(scores - top)
    total = jnp.sum(weights, axis=-1, keepdims=True)
    low_probs = (weights / total).astype(jnp.bfloat16)
    context = jnp.einsum(
        "bhqk,bkhd->bqhd",
        low_probs,
        split_heads(value_rows, heads),
        preferred_element_type=jnp.float32,
    )
    return (context.reshape(query_rows.shape[0], -1).astype(jnp.bfloat16), top + jnp.log(total))


def attend_back(query_rows, key_rows, value_rows, log_total, context_grad, heads):
    factor = DH ** (-0.5)
    query_heads = split_heads(query_rows, heads)
    key_heads = split_heads(key_rows, heads)
    value_heads = split_heads(value_rows, heads)
    grad_heads = split_heads(context_grad, heads)
    scores = (
        jnp.einsum("bqhd,bkhd->bhqk", query_heads, key_heads, preferred_element_type=jnp.float32)
        * factor
    )
    probs = jnp.exp(scores - log_total)
    low_probs = probs.astype(jnp.bfloat16)
    value_grad = jnp.einsum(
        "bhqk,bqhd->bkhd", low_probs, grad_heads, preferred_element_type=jnp.float32
    )
    prob_grad = jnp.einsum(
        "bqhd,bkhd->bhqk", grad_heads, value_heads, preferred_element_type=jnp.float32
    )
    inner_sum = jnp.sum(probs * prob_grad, axis=-1, keepdims=True)
    score_grad = (probs * (prob_grad - inner_sum)).astype(jnp.bfloat16)
    query_grad = (
        jnp.einsum("bhqk,bkhd->bqhd", score_grad, key_heads, preferred_element_type=jnp.float32)
        * factor
    )
    key_grad = (
        jnp.einsum("bhqk,bqhd->bkhd", score_grad, query_heads, preferred_element_type=jnp.float32)
        * factor
    )
    count = query_rows.shape[0]
    joined = jnp.concatenate(
        [query_grad.reshape(count, -1), key_grad.reshape(count, -1), value_grad.reshape(count, -1)],
        axis=1,
    )
    return joined.astype(jnp.bfloat16)


def local(
    inputs,
    query_weight,
    query_bias,
    key_weight,
    value_weight,
    value_bias,
    mixer_weight,
    mixer_bias,
    norm_gain,
    norm_bias,
    inner_weight,
    inner_bias,
    outer_weight,
    outer_bias,
    final_gain,
    final_bias,
    cotangent,
):
    head_width = query_weight.shape[1]
    heads = head_width // DH
    row_at, col_at = lax.axis_index("row"), lax.axis_index("col")
    chunk = inputs.shape[0] // lax.axis_size("row")
    width = inputs.shape[1]

    input_all = lax.all_gather(transposed(inputs), "row", axis=1, tiled=True)
    attention_weights = cols_gather(
        jnp.concatenate([query_weight, key_weight, value_weight, mixer_weight.T], axis=1)
    )
    joint_weight = attention_weights[:, : 3 * head_width]
    mixer_turned = attention_weights[:, 3 * head_width :]
    inner_full = cols_gather(inner_weight)
    outer_turned = cols_gather(outer_weight.T)
    vectors = lax.all_gather(
        jnp.stack([mixer_bias, norm_gain, norm_bias, outer_bias, final_gain, final_bias]),
        "col",
        axis=1,
        tiled=True,
    )
    mixer_bias, norm_gain, norm_bias, outer_bias, final_gain, final_bias = (
        vectors[i] for i in range(6)
    )
    upstream = lax.all_to_all(
        transposed(cotangent), "row", split_axis=0, concat_axis=1, tiled=True
    ).astype(jnp.float32)

    input_own = lax.dynamic_slice_in_dim(input_all, row_at * chunk, chunk, axis=0)
    projected = multiply(input_all, joint_weight, False)
    query_rows = (projected[:, :head_width] + query_bias).astype(jnp.bfloat16)
    key_rows = projected[:, head_width : 2 * head_width].astype(jnp.bfloat16)
    value_rows = (projected[:, 2 * head_width :] + value_bias).astype(jnp.bfloat16)
    context, log_total = attend(query_rows, key_rows, value_rows, heads)
    mixed = row_reduce(multiply(context, mixer_turned, True)).astype(jnp.float32)
    first_sum = input_own.astype(jnp.float32) + mixed + mixer_bias
    first_hat, first_scale = normalize(first_sum)
    first_out = first_hat * norm_gain + norm_bias
    mid_all = rows_gather(first_out.astype(jnp.bfloat16))
    inner_pre = multiply(mid_all, inner_full, False) + inner_bias
    activated = jax.nn.gelu(inner_pre, approximate=False).astype(jnp.bfloat16)
    outer = row_reduce(multiply(activated, outer_turned, True)).astype(jnp.float32)
    second_sum = first_out + outer + outer_bias
    second_hat, second_scale = normalize(second_sum)
    layer_rows = (second_hat * final_gain + final_bias).astype(jnp.bfloat16)
    layer_out = transposed(
        lax.all_to_all(layer_rows, "row", split_axis=1, concat_axis=0, tiled=True)
    )
    grad_finalgain = jnp.sum(upstream * second_hat, axis=0)
    grad_finalbias = jnp.sum(upstream, axis=0)
    second_grad = norm_back(upstream * final_gain, second_hat, second_scale)
    second_low = second_grad.astype(jnp.bfloat16)
    grad_outerbias = column_sums(second_low)
    second_all = rows_gather(second_low)
    act_grad = multiply(second_all, outer_turned, False)
    inner_grad = (act_grad * gelu_slope(inner_pre)).astype(jnp.bfloat16)
    mid_grad = row_reduce(multiply(inner_grad, inner_full, True)).astype(jnp.float32)
    grad_outerweight = grad_reduce(outer_product(second_all, activated)).T
    grad_innerbias = column_sums(inner_grad)
    grad_innerweight = grad_reduce(outer_product(mid_all, inner_grad))
    first_up = second_grad + mid_grad
    grad_normgain = jnp.sum(first_up * first_hat, axis=0)
    grad_normbias = jnp.sum(first_up, axis=0)
    first_grad = norm_back(first_up * norm_gain, first_hat, first_scale)
    first_low = first_grad.astype(jnp.bfloat16)
    grad_mixerbias = column_sums(first_low)
    first_all = rows_gather(first_low)
    context_grad = multiply(first_all, mixer_turned, False).astype(jnp.bfloat16)
    joint_grad = attend_back(query_rows, key_rows, value_rows, log_total, context_grad, heads)
    input_part = multiply(joint_grad, joint_weight, True)
    own_part = lax.dynamic_slice_in_dim(input_part, row_at * chunk, chunk, axis=0) + first_grad
    input_part = lax.dynamic_update_slice_in_dim(input_part, own_part, row_at * chunk, axis=0)
    grad_inputs = transposed(row_reduce(input_part, 1)).astype(jnp.float32)
    joint_bias = column_sums(joint_grad)
    grad_attention = grad_reduce(
        jnp.concatenate(
            [outer_product(input_all, joint_grad), outer_product(first_all, context)], axis=1
        )
    )
    grad_joint = grad_attention[:, : 3 * head_width]
    grad_mixerweight = grad_attention[:, 3 * head_width :].T
    grad_innerbias, joint_bias = lax.psum((grad_innerbias, joint_bias), ("dp", "col"))
    sums = lax.psum(
        jnp.stack(
            [
                grad_normgain,
                grad_normbias,
                grad_finalgain,
                grad_finalbias,
                grad_mixerbias,
                grad_outerbias,
            ]
        ),
        ("dp", "row", "col"),
    )
    sums = lax.dynamic_slice_in_dim(sums, col_at * width, width, axis=1)
    grad_normgain, grad_normbias, grad_finalgain, grad_finalbias, grad_mixerbias, grad_outerbias = (
        sums[i] for i in range(6)
    )
    grad_queryweight = grad_joint[:, :head_width]
    grad_keyweight = grad_joint[:, head_width : 2 * head_width]
    grad_valueweight = grad_joint[:, 2 * head_width :]
    grad_querybias = joint_bias[:head_width]
    grad_valuebias = joint_bias[2 * head_width :]
    return (
        layer_out,
        grad_inputs,
        grad_queryweight,
        grad_querybias,
        grad_keyweight,
        grad_valueweight,
        grad_valuebias,
        grad_mixerweight,
        grad_mixerbias,
        grad_normgain,
        grad_normbias,
        grad_innerweight,
        grad_innerbias,
        grad_outerweight,
        grad_outerbias,
        grad_finalgain,
        grad_finalbias,
    )


def solution(mesh):
    return jax.shard_map(
        local,
        mesh=mesh,
        in_specs=(
            P(("dp", "row"), "col"),
            P("col", "row"),
            P("row"),
            P("col", "row"),
            P("col", "row"),
            P("row"),
            P("row", "col"),
            P("col"),
            P("col"),
            P("col"),
            P("col", "row"),
            P("row"),
            P("row", "col"),
            P("col"),
            P("col"),
            P("col"),
            P(("dp", "row"), "col"),
        ),
        out_specs=(
            P(("dp", "row"), "col"),
            P(("dp", "row"), "col"),
            P("col", "row"),
            P("row"),
            P("col", "row"),
            P("col", "row"),
            P("row"),
            P("row", "col"),
            P("col"),
            P("col"),
            P("col"),
            P("col", "row"),
            P("row"),
            P("row", "col"),
            P("col"),
            P("col"),
            P("col"),
        ),
        check_vma=False,
    )
```

```python
import math

import jax
import jax.numpy as jnp
from jax import lax
from jax.sharding import PartitionSpec as P

D = 1024
DH = 64
L = 512


norm_eps = 1e-12


def multiply(left, right, flipped):
    if flipped:
        return lax.dot_general(
            left, right, (((1,), (1,)), ((), ())), preferred_element_type=jnp.float32
        )
    return jnp.dot(left, right, preferred_element_type=jnp.float32)


def outer_product(left, right):
    return lax.dot_general(
        left, right, (((0,), (0,)), ((), ())), preferred_element_type=jnp.float32
    )


def column_sums(block):
    return jnp.dot(
        jnp.ones((1, block.shape[0]), block.dtype), block, preferred_element_type=jnp.float32
    )[0]


def flipped_axis(block, axis, mask):
    return lax.ppermute(block, axis, [(i, i ^ mask) for i in range(lax.axis_size(axis))])


def cols_gather(block):
    return lax.all_gather(block, "col", axis=0, tiled=True)


def rows_gather(block):
    chunks = {0: block}
    mask = lax.axis_size("row") // 2
    while mask:
        held = sorted(chunks)
        arrived = flipped_axis(jnp.concatenate([chunks[m] for m in held]), "row", mask)
        for m, part in zip(held, jnp.split(arrived, len(held))):
            chunks[m ^ mask] = part
        mask //= 2
    return jnp.concatenate([chunks[m] for m in sorted(chunks)])


def row_reduce(partial):
    count = lax.axis_size("row")
    chunks = dict(enumerate(jnp.split(partial, count)))
    mask = 1
    while mask < count:
        away = [m for m in sorted(chunks) if m & mask]
        arrived = flipped_axis(
            jnp.concatenate([chunks[m] for m in away]).astype(jnp.bfloat16), "row", mask
        )
        for m, part in zip(away, jnp.split(arrived, len(away))):
            chunks[m ^ mask] = chunks[m ^ mask] + part.astype(jnp.float32)
            del chunks[m]
        mask *= 2
    return chunks[0]


def in_order(parts, at, axis):
    stacked = jnp.stack(parts)
    return jnp.concatenate(
        [
            lax.dynamic_index_in_dim(stacked, at ^ i, axis=0, keepdims=False)
            for i in range(len(parts))
        ],
        axis=axis,
    )


def to_whole_rows(block):
    count = lax.axis_size("row")
    row_at, col_at = lax.axis_index("row"), lax.axis_index("col")
    chunks = jnp.stack(jnp.split(block, count))
    parts = []
    for k in range(count):
        sent = lax.dynamic_index_in_dim(chunks, col_at ^ k, axis=0, keepdims=False)
        pairs = [(r * count + c, (c ^ k) * count + r) for r in range(count) for c in range(count)]
        parts.append(lax.ppermute(sent, ("row", "col"), pairs))
    return in_order(parts, row_at, 1)


def to_feature_blocks(rows):
    count = lax.axis_size("row")
    row_at, col_at = lax.axis_index("row"), lax.axis_index("col")
    blocks = jnp.stack(jnp.split(rows, count, axis=1))
    parts = []
    for k in range(count):
        sent = lax.dynamic_index_in_dim(blocks, row_at ^ k, axis=0, keepdims=False)
        pairs = [(r * count + c, c * count + (r ^ k)) for r in range(count) for c in range(count)]
        parts.append(lax.ppermute(sent, ("row", "col"), pairs))
    return in_order(parts, col_at, 0)


def butterfly_sum(values, axis):
    mask = 1
    while mask < lax.axis_size(axis):
        values = values + flipped_axis(values, axis, mask)
        mask *= 2
    return values


def replica_sum(values):
    if lax.axis_size("dp") == 2:
        return values.astype(jnp.float32) + flipped_axis(values, "dp", 1).astype(jnp.float32)
    return lax.psum(values, "dp").astype(jnp.float32)


def grad_reduce(partial):
    return replica_sum(
        lax.psum_scatter(partial.astype(jnp.bfloat16), "col", scatter_dimension=0, tiled=True)
    )


def normalize(total):
    center = jnp.mean(total, axis=-1, keepdims=True)
    moved = total - center
    scale = lax.rsqrt(jnp.mean(moved * moved, axis=-1, keepdims=True) + norm_eps)
    return moved * scale, scale


def norm_back(scaled_grad, normed, scale):
    first = jnp.mean(scaled_grad, axis=-1, keepdims=True)
    second = jnp.mean(scaled_grad * normed, axis=-1, keepdims=True)
    return scale * (scaled_grad - first - normed * second)


def gelu_slope(values):
    normal_cdf = 0.5 * (1.0 + jax.scipy.special.erf(values * (1.0 / math.sqrt(2.0))))
    density = jnp.exp(-0.5 * values * values) * (1.0 / math.sqrt(2.0 * math.pi))
    return normal_cdf + values * density


def split_heads(block, heads):
    return block.reshape(-1, L, heads, DH)


def attend(query_rows, key_rows, value_rows, heads):
    factor = DH ** (-0.5)
    scores = (
        jnp.einsum(
            "bqhd,bkhd->bhqk",
            split_heads(query_rows, heads),
            split_heads(key_rows, heads),
            preferred_element_type=jnp.float32,
        )
        * factor
    )
    top = jnp.max(scores, axis=-1, keepdims=True)
    weights = jnp.exp(scores - top)
    total = jnp.sum(weights, axis=-1, keepdims=True)
    low_probs = (weights / total).astype(jnp.bfloat16)
    context = jnp.einsum(
        "bhqk,bkhd->bqhd",
        low_probs,
        split_heads(value_rows, heads),
        preferred_element_type=jnp.float32,
    )
    return (context.reshape(query_rows.shape[0], -1).astype(jnp.bfloat16), top + jnp.log(total))


def attend_back(query_rows, key_rows, value_rows, log_total, context_grad, heads):
    factor = DH ** (-0.5)
    query_heads = split_heads(query_rows, heads)
    key_heads = split_heads(key_rows, heads)
    value_heads = split_heads(value_rows, heads)
    grad_heads = split_heads(context_grad, heads)
    scores = (
        jnp.einsum("bqhd,bkhd->bhqk", query_heads, key_heads, preferred_element_type=jnp.float32)
        * factor
    )
    probs = jnp.exp(scores - log_total)
    low_probs = probs.astype(jnp.bfloat16)
    value_grad = jnp.einsum(
        "bhqk,bqhd->bkhd", low_probs, grad_heads, preferred_element_type=jnp.float32
    )
    prob_grad = jnp.einsum(
        "bqhd,bkhd->bhqk", grad_heads, value_heads, preferred_element_type=jnp.float32
    )
    inner_sum = jnp.sum(probs * prob_grad, axis=-1, keepdims=True)
    score_grad = (probs * (prob_grad - inner_sum)).astype(jnp.bfloat16)
    query_grad = (
        jnp.einsum("bhqk,bkhd->bqhd", score_grad, key_heads, preferred_element_type=jnp.float32)
        * factor
    )
    key_grad = (
        jnp.einsum("bhqk,bqhd->bkhd", score_grad, query_heads, preferred_element_type=jnp.float32)
        * factor
    )
    count = query_rows.shape[0]
    joined = jnp.concatenate(
        [query_grad.reshape(count, -1), key_grad.reshape(count, -1), value_grad.reshape(count, -1)],
        axis=1,
    )
    return joined.astype(jnp.bfloat16)


def local(
    inputs,
    query_weight,
    query_bias,
    key_weight,
    value_weight,
    value_bias,
    mixer_weight,
    mixer_bias,
    norm_gain,
    norm_bias,
    inner_weight,
    inner_bias,
    outer_weight,
    outer_bias,
    final_gain,
    final_bias,
    cotangent,
):
    head_width = query_weight.shape[1]
    heads = head_width // DH
    col_at = lax.axis_index("col")
    width = inputs.shape[1]

    input_own = to_whole_rows(inputs)
    input_all = rows_gather(input_own)
    joint_weight = cols_gather(jnp.concatenate([query_weight, key_weight, value_weight], axis=1))
    inner_group = cols_gather(jnp.concatenate([mixer_weight.T, inner_weight], axis=1))
    mixer_turned = inner_group[:, :head_width]
    inner_full = inner_group[:, head_width:]
    outer_turned = cols_gather(outer_weight.T)
    vectors = jnp.stack([mixer_bias, norm_gain, norm_bias, outer_bias, final_gain, final_bias])
    vectors = in_order(
        [vectors] + [flipped_axis(vectors, "col", k) for k in range(1, lax.axis_size("col"))],
        col_at,
        1,
    )
    mixer_bias, norm_gain, norm_bias, outer_bias, final_gain, final_bias = (
        vectors[i] for i in range(6)
    )
    upstream = to_whole_rows(cotangent).astype(jnp.float32)

    projected = multiply(input_all, joint_weight, False)
    query_rows = (projected[:, :head_width] + query_bias).astype(jnp.bfloat16)
    key_rows = projected[:, head_width : 2 * head_width].astype(jnp.bfloat16)
    value_rows = (projected[:, 2 * head_width :] + value_bias).astype(jnp.bfloat16)
    context, log_total = attend(query_rows, key_rows, value_rows, heads)
    mixed = row_reduce(multiply(context, mixer_turned, True))
    first_sum = input_own.astype(jnp.float32) + mixed + mixer_bias
    first_hat, first_scale = normalize(first_sum)
    first_out = first_hat * norm_gain + norm_bias
    mid_all = rows_gather(first_out.astype(jnp.bfloat16))
    inner_pre = multiply(mid_all, inner_full, False) + inner_bias
    activated = jax.nn.gelu(inner_pre, approximate=False).astype(jnp.bfloat16)
    outer = row_reduce(multiply(activated, outer_turned, True))
    second_sum = first_out + outer + outer_bias
    second_hat, second_scale = normalize(second_sum)
    layer_rows = (second_hat * final_gain + final_bias).astype(jnp.bfloat16)
    layer_out = to_feature_blocks(layer_rows)
    grad_finalgain = jnp.sum(upstream * second_hat, axis=0)
    grad_finalbias = jnp.sum(upstream, axis=0)
    second_grad = norm_back(upstream * final_gain, second_hat, second_scale)
    second_low = second_grad.astype(jnp.bfloat16)
    grad_outerbias = column_sums(second_low)
    second_all = rows_gather(second_low)
    act_grad = multiply(second_all, outer_turned, False)
    inner_grad = (act_grad * gelu_slope(inner_pre)).astype(jnp.bfloat16)
    mid_grad = row_reduce(multiply(inner_grad, inner_full, True))
    grad_outerweight = grad_reduce(outer_product(second_all, activated)).T
    grad_innerbias = column_sums(inner_grad)
    grad_innerweight = grad_reduce(outer_product(mid_all, inner_grad))
    first_up = second_grad + mid_grad
    grad_normgain = jnp.sum(first_up * first_hat, axis=0)
    grad_normbias = jnp.sum(first_up, axis=0)
    first_grad = norm_back(first_up * norm_gain, first_hat, first_scale)
    first_low = first_grad.astype(jnp.bfloat16)
    grad_mixerbias = column_sums(first_low)
    first_all = rows_gather(first_low)
    context_grad = multiply(first_all, mixer_turned, False).astype(jnp.bfloat16)
    joint_grad = attend_back(query_rows, key_rows, value_rows, log_total, context_grad, heads)
    input_grad = first_grad + row_reduce(multiply(joint_grad, joint_weight, True))
    grad_inputs = to_feature_blocks(input_grad.astype(jnp.bfloat16)).astype(jnp.float32)
    joint_bias = column_sums(joint_grad)
    grad_attention = grad_reduce(
        jnp.concatenate(
            [outer_product(input_all, joint_grad), outer_product(first_all, context)], axis=1
        )
    )
    grad_joint = grad_attention[:, : 3 * head_width]
    grad_mixerweight = grad_attention[:, 3 * head_width :].T
    row_sums = [
        grad_normgain,
        grad_normbias,
        grad_finalgain,
        grad_finalbias,
        grad_mixerbias,
        grad_outerbias,
    ]
    sums = replica_sum(
        butterfly_sum(jnp.concatenate(row_sums + [grad_innerbias, joint_bias]), "col")
    )
    split_at = 6 * D
    grad_innerbias = sums[split_at : split_at + grad_innerbias.shape[0]]
    joint_bias = sums[split_at + grad_innerbias.shape[0] :]
    sums = lax.dynamic_slice_in_dim(
        sums[:split_at].reshape(6, D), col_at * width, width, axis=1
    )
    sums = butterfly_sum(sums, "row")
    grad_normgain, grad_normbias, grad_finalgain, grad_finalbias, grad_mixerbias, grad_outerbias = (
        sums[i] for i in range(6)
    )
    grad_queryweight = grad_joint[:, :head_width]
    grad_keyweight = grad_joint[:, head_width : 2 * head_width]
    grad_valueweight = grad_joint[:, 2 * head_width :]
    grad_querybias = joint_bias[:head_width]
    grad_valuebias = joint_bias[2 * head_width :]
    return (
        layer_out,
        grad_inputs,
        grad_queryweight,
        grad_querybias,
        grad_keyweight,
        grad_valueweight,
        grad_valuebias,
        grad_mixerweight,
        grad_mixerbias,
        grad_normgain,
        grad_normbias,
        grad_innerweight,
        grad_innerbias,
        grad_outerweight,
        grad_outerbias,
        grad_finalgain,
        grad_finalbias,
    )


def solution(mesh):
    return jax.shard_map(
        local,
        mesh=mesh,
        in_specs=(
            P(("dp", "row"), "col"),
            P("col", "row"),
            P("row"),
            P("col", "row"),
            P("col", "row"),
            P("row"),
            P("row", "col"),
            P("col"),
            P("col"),
            P("col"),
            P("col", "row"),
            P("row"),
            P("row", "col"),
            P("col"),
            P("col"),
            P("col"),
            P(("dp", "row"), "col"),
        ),
        out_specs=(
            P(("dp", "row"), "col"),
            P(("dp", "row"), "col"),
            P("col", "row"),
            P("row"),
            P("col", "row"),
            P("col", "row"),
            P("row"),
            P("row", "col"),
            P("col"),
            P("col"),
            P("col"),
            P("col", "row"),
            P("row"),
            P("row", "col"),
            P("col"),
            P("col"),
            P("col"),
        ),
        check_vma=False,
    )
```

```python
import math

import jax
import jax.numpy as jnp
from jax import lax
from jax.sharding import PartitionSpec as P

D = 1024
DH = 64
L = 512


norm_eps = 1e-12


def multiply(left, right, flipped):
    if flipped:
        return lax.dot_general(
            left, right, (((1,), (1,)), ((), ())), preferred_element_type=jnp.float32
        )
    return jnp.dot(left, right, preferred_element_type=jnp.float32)


def outer_product(left, right):
    return lax.dot_general(
        left, right, (((0,), (0,)), ((), ())), preferred_element_type=jnp.float32
    )


def column_sums(block):
    return jnp.dot(
        jnp.ones((1, block.shape[0]), block.dtype), block, preferred_element_type=jnp.float32
    )[0]


def flipped_axis(block, axis, mask):
    return lax.ppermute(block, axis, [(i, i ^ mask) for i in range(lax.axis_size(axis))])


def cols_gather(block):
    if lax.axis_size("dp") == 2:
        half = block.shape[0] // 2
        block = lax.dynamic_slice_in_dim(block, lax.axis_index("dp") * half, half, axis=0)
    return lax.all_gather(block, "col", axis=0, tiled=False)


def replicas_join(gathered):
    if lax.axis_size("dp") == 2:
        other = flipped_axis(gathered, "dp", 1)
        first = lax.axis_index("dp") == 0
        gathered = jnp.stack(
            [jnp.where(first, gathered, other), jnp.where(first, other, gathered)], axis=1
        )
    return gathered.reshape(-1, gathered.shape[-1])


def rows_gather(block):
    chunks = {0: block}
    mask = lax.axis_size("row") // 2
    while mask:
        held = sorted(chunks)
        arrived = flipped_axis(jnp.concatenate([chunks[m] for m in held]), "row", mask)
        for m, part in zip(held, jnp.split(arrived, len(held))):
            chunks[m ^ mask] = part
        mask //= 2
    return jnp.concatenate([chunks[m] for m in sorted(chunks)])


def row_reduce(partial):
    count = lax.axis_size("row")
    chunks = dict(enumerate(jnp.split(partial, count)))
    mask = 1
    while mask < count:
        away = [m for m in sorted(chunks) if m & mask]
        arrived = flipped_axis(
            jnp.concatenate([chunks[m] for m in away]).astype(jnp.bfloat16), "row", mask
        )
        for m, part in zip(away, jnp.split(arrived, len(away))):
            chunks[m ^ mask] = chunks[m ^ mask] + part.astype(jnp.float32)
            del chunks[m]
        mask *= 2
    return chunks[0]


def in_order(parts, at, axis):
    stacked = jnp.stack(parts)
    return jnp.concatenate(
        [
            lax.dynamic_index_in_dim(stacked, at ^ i, axis=0, keepdims=False)
            for i in range(len(parts))
        ],
        axis=axis,
    )


def to_whole_rows(block):
    count = lax.axis_size("row")
    row_at, col_at = lax.axis_index("row"), lax.axis_index("col")
    chunks = jnp.stack(jnp.split(block, count))
    parts = []
    for k in range(count):
        sent = lax.dynamic_index_in_dim(chunks, col_at ^ k, axis=0, keepdims=False)
        pairs = [(r * count + c, (c ^ k) * count + r) for r in range(count) for c in range(count)]
        parts.append(lax.ppermute(sent, ("row", "col"), pairs))
    return in_order(parts, row_at, 1)


def to_feature_blocks(rows):
    count = lax.axis_size("row")
    row_at, col_at = lax.axis_index("row"), lax.axis_index("col")
    blocks = jnp.stack(jnp.split(rows, count, axis=1))
    parts = []
    for k in range(count):
        sent = lax.dynamic_index_in_dim(blocks, row_at ^ k, axis=0, keepdims=False)
        pairs = [(r * count + c, c * count + (r ^ k)) for r in range(count) for c in range(count)]
        parts.append(lax.ppermute(sent, ("row", "col"), pairs))
    return in_order(parts, col_at, 0)


def butterfly_sum(values, axis):
    mask = 1
    while mask < lax.axis_size(axis):
        values = values + flipped_axis(values, axis, mask)
        mask *= 2
    return values


def replica_sum(values):
    if lax.axis_size("dp") == 2:
        return values.astype(jnp.float32) + flipped_axis(values, "dp", 1).astype(jnp.float32)
    return lax.psum(values, "dp").astype(jnp.float32)


def grad_reduce(partial):
    return replica_sum(
        lax.psum_scatter(partial.astype(jnp.bfloat16), "col", scatter_dimension=0, tiled=True)
    )


def normalize(total):
    center = jnp.mean(total, axis=-1, keepdims=True)
    moved = total - center
    scale = lax.rsqrt(jnp.mean(moved * moved, axis=-1, keepdims=True) + norm_eps)
    return moved * scale, scale


def norm_back(scaled_grad, normed, scale):
    first = jnp.mean(scaled_grad, axis=-1, keepdims=True)
    second = jnp.mean(scaled_grad * normed, axis=-1, keepdims=True)
    return scale * (scaled_grad - first - normed * second)


def gelu_slope(values):
    normal_cdf = 0.5 * (1.0 + jax.scipy.special.erf(values * (1.0 / math.sqrt(2.0))))
    density = jnp.exp(-0.5 * values * values) * (1.0 / math.sqrt(2.0 * math.pi))
    return normal_cdf + values * density


def split_heads(block, heads):
    return block.reshape(-1, L, heads, DH)


def attend(query_rows, key_rows, value_rows, heads):
    factor = DH ** (-0.5)
    scores = (
        jnp.einsum(
            "bqhd,bkhd->bhqk",
            split_heads(query_rows, heads),
            split_heads(key_rows, heads),
            preferred_element_type=jnp.float32,
        )
        * factor
    )
    top = jnp.max(scores, axis=-1, keepdims=True)
    weights = jnp.exp(scores - top)
    total = jnp.sum(weights, axis=-1, keepdims=True)
    low_probs = (weights / total).astype(jnp.bfloat16)
    context = jnp.einsum(
        "bhqk,bkhd->bqhd",
        low_probs,
        split_heads(value_rows, heads),
        preferred_element_type=jnp.float32,
    )
    return (context.reshape(query_rows.shape[0], -1).astype(jnp.bfloat16), top + jnp.log(total))


def attend_back(query_rows, key_rows, value_rows, log_total, context_grad, heads):
    factor = DH ** (-0.5)
    query_heads = split_heads(query_rows, heads)
    key_heads = split_heads(key_rows, heads)
    value_heads = split_heads(value_rows, heads)
    grad_heads = split_heads(context_grad, heads)
    scores = (
        jnp.einsum("bqhd,bkhd->bhqk", query_heads, key_heads, preferred_element_type=jnp.float32)
        * factor
    )
    probs = jnp.exp(scores - log_total)
    low_probs = probs.astype(jnp.bfloat16)
    value_grad = jnp.einsum(
        "bhqk,bqhd->bkhd", low_probs, grad_heads, preferred_element_type=jnp.float32
    )
    prob_grad = jnp.einsum(
        "bqhd,bkhd->bhqk", grad_heads, value_heads, preferred_element_type=jnp.float32
    )
    inner_sum = jnp.sum(probs * prob_grad, axis=-1, keepdims=True)
    score_grad = (probs * (prob_grad - inner_sum)).astype(jnp.bfloat16)
    query_grad = (
        jnp.einsum("bhqk,bkhd->bqhd", score_grad, key_heads, preferred_element_type=jnp.float32)
        * factor
    )
    key_grad = (
        jnp.einsum("bhqk,bqhd->bkhd", score_grad, query_heads, preferred_element_type=jnp.float32)
        * factor
    )
    count = query_rows.shape[0]
    joined = jnp.concatenate(
        [query_grad.reshape(count, -1), key_grad.reshape(count, -1), value_grad.reshape(count, -1)],
        axis=1,
    )
    return joined.astype(jnp.bfloat16)


def local(
    inputs,
    query_weight,
    query_bias,
    key_weight,
    value_weight,
    value_bias,
    mixer_weight,
    mixer_bias,
    norm_gain,
    norm_bias,
    inner_weight,
    inner_bias,
    outer_weight,
    outer_bias,
    final_gain,
    final_bias,
    cotangent,
):
    head_width = query_weight.shape[1]
    heads = head_width // DH
    col_at = lax.axis_index("col")
    width = inputs.shape[1]

    input_own = to_whole_rows(inputs)
    input_all = rows_gather(input_own)
    attention_part = cols_gather(
        jnp.concatenate([query_weight, key_weight, value_weight, mixer_weight.T], axis=1)
    )
    inner_part = cols_gather(inner_weight)
    outer_part = cols_gather(outer_weight.T)
    attention_weights = replicas_join(attention_part)
    input_all, inner_part = lax.optimization_barrier((input_all, inner_part))
    joint_weight = attention_weights[:, : 3 * head_width]
    mixer_turned = attention_weights[:, 3 * head_width :]
    inner_full = replicas_join(inner_part)
    vectors = jnp.stack([mixer_bias, norm_gain, norm_bias, outer_bias, final_gain, final_bias])
    vectors = in_order(
        [vectors] + [flipped_axis(vectors, "col", k) for k in range(1, lax.axis_size("col"))],
        col_at,
        1,
    )
    mixer_bias, norm_gain, norm_bias, outer_bias, final_gain, final_bias = (
        vectors[i] for i in range(6)
    )
    upstream = to_whole_rows(cotangent).astype(jnp.float32)

    projected = multiply(input_all, joint_weight, False)
    query_rows = (projected[:, :head_width] + query_bias).astype(jnp.bfloat16)
    key_rows = projected[:, head_width : 2 * head_width].astype(jnp.bfloat16)
    value_rows = (projected[:, 2 * head_width :] + value_bias).astype(jnp.bfloat16)
    context, log_total = attend(query_rows, key_rows, value_rows, heads)
    context, outer_part, inner_full = lax.optimization_barrier((context, outer_part, inner_full))
    outer_turned = replicas_join(outer_part)
    mixed = row_reduce(multiply(context, mixer_turned, True))
    first_sum = input_own.astype(jnp.float32) + mixed + mixer_bias
    first_hat, first_scale = normalize(first_sum)
    first_out = first_hat * norm_gain + norm_bias
    mid_all = rows_gather(first_out.astype(jnp.bfloat16))
    inner_pre = multiply(mid_all, inner_full, False) + inner_bias
    activated = jax.nn.gelu(inner_pre, approximate=False).astype(jnp.bfloat16)
    outer = row_reduce(multiply(activated, outer_turned, True))
    second_sum = first_out + outer + outer_bias
    second_hat, second_scale = normalize(second_sum)
    layer_rows = (second_hat * final_gain + final_bias).astype(jnp.bfloat16)
    layer_out = to_feature_blocks(layer_rows)
    grad_finalgain = jnp.sum(upstream * second_hat, axis=0)
    grad_finalbias = jnp.sum(upstream, axis=0)
    second_grad = norm_back(upstream * final_gain, second_hat, second_scale)
    second_low = second_grad.astype(jnp.bfloat16)
    grad_outerbias = column_sums(second_low)
    second_all = rows_gather(second_low)
    act_grad = multiply(second_all, outer_turned, False)
    inner_grad = (act_grad * gelu_slope(inner_pre)).astype(jnp.bfloat16)
    mid_grad = row_reduce(multiply(inner_grad, inner_full, True))
    grad_outerweight = grad_reduce(outer_product(second_all, activated)).T
    grad_innerbias = column_sums(inner_grad)
    grad_innerweight = grad_reduce(outer_product(mid_all, inner_grad))
    first_up = second_grad + mid_grad
    grad_normgain = jnp.sum(first_up * first_hat, axis=0)
    grad_normbias = jnp.sum(first_up, axis=0)
    first_grad = norm_back(first_up * norm_gain, first_hat, first_scale)
    first_low = first_grad.astype(jnp.bfloat16)
    grad_mixerbias = column_sums(first_low)
    first_all = rows_gather(first_low)
    context_grad = multiply(first_all, mixer_turned, False).astype(jnp.bfloat16)
    joint_grad = attend_back(query_rows, key_rows, value_rows, log_total, context_grad, heads)
    input_grad = first_grad + row_reduce(multiply(joint_grad, joint_weight, True))
    grad_inputs = to_feature_blocks(input_grad.astype(jnp.bfloat16)).astype(jnp.float32)
    joint_bias = column_sums(joint_grad)
    grad_attention = grad_reduce(
        jnp.concatenate(
            [outer_product(input_all, joint_grad), outer_product(first_all, context)], axis=1
        )
    )
    grad_joint = grad_attention[:, : 3 * head_width]
    grad_mixerweight = grad_attention[:, 3 * head_width :].T
    row_sums = [
        grad_normgain,
        grad_normbias,
        grad_finalgain,
        grad_finalbias,
        grad_mixerbias,
        grad_outerbias,
    ]
    sums = replica_sum(
        butterfly_sum(jnp.concatenate(row_sums + [grad_innerbias, joint_bias]), "col")
    )
    split_at = 6 * D
    grad_innerbias = sums[split_at : split_at + grad_innerbias.shape[0]]
    joint_bias = sums[split_at + grad_innerbias.shape[0] :]
    sums = lax.dynamic_slice_in_dim(
        sums[:split_at].reshape(6, D), col_at * width, width, axis=1
    )
    sums = butterfly_sum(sums, "row")
    grad_normgain, grad_normbias, grad_finalgain, grad_finalbias, grad_mixerbias, grad_outerbias = (
        sums[i] for i in range(6)
    )
    grad_queryweight = grad_joint[:, :head_width]
    grad_keyweight = grad_joint[:, head_width : 2 * head_width]
    grad_valueweight = grad_joint[:, 2 * head_width :]
    grad_querybias = joint_bias[:head_width]
    grad_valuebias = joint_bias[2 * head_width :]
    return (
        layer_out,
        grad_inputs,
        grad_queryweight,
        grad_querybias,
        grad_keyweight,
        grad_valueweight,
        grad_valuebias,
        grad_mixerweight,
        grad_mixerbias,
        grad_normgain,
        grad_normbias,
        grad_innerweight,
        grad_innerbias,
        grad_outerweight,
        grad_outerbias,
        grad_finalgain,
        grad_finalbias,
    )


def solution(mesh):
    return jax.shard_map(
        local,
        mesh=mesh,
        in_specs=(
            P(("dp", "row"), "col"),
            P("col", "row"),
            P("row"),
            P("col", "row"),
            P("col", "row"),
            P("row"),
            P("row", "col"),
            P("col"),
            P("col"),
            P("col"),
            P("col", "row"),
            P("row"),
            P("row", "col"),
            P("col"),
            P("col"),
            P("col"),
            P(("dp", "row"), "col"),
        ),
        out_specs=(
            P(("dp", "row"), "col"),
            P(("dp", "row"), "col"),
            P("col", "row"),
            P("row"),
            P("col", "row"),
            P("col", "row"),
            P("row"),
            P("row", "col"),
            P("col"),
            P("col"),
            P("col"),
            P("col", "row"),
            P("row"),
            P("row", "col"),
            P("col"),
            P("col"),
            P("col"),
        ),
        check_vma=False,
    )
```
